32 devices in a mesh: groups: 2 (over x), dp: 16 (over z, y, core), tensor: 1.
Axes of the slice: x: 2, y: 2, z: 4, core: 2. Of those that a mesh axis runs over, the one named last changes fastest.
Arguments:
- token_rows: bfloat16 [512, 7168], P(('groups', 'dp', 'tensor')), parts along dimension 0, may hold values from -6 to 6
- expert_ids: int32 [512, 2], P(('groups', 'dp', 'tensor')), parts along dimension 0, may hold values from 0 to 3, all different within a row; in each aligned block of 16 rows (0 to 15, 16 to 31, ...) at most 16 rows name the same one
- gate_weights: float32 [512, 2], P(('groups', 'dp', 'tensor')), parts along dimension 0, may hold values from 0.2 to 1
- cap_limit: int32 [8], P('groups'), parts along dimension 0, may hold values from 8 to 16, as said below
- queries: bfloat16 [64, 128, 576], P(('groups', 'dp'), 'tensor'), parts along dimension 0, may hold values from -80 to 80
- latent_cache: bfloat16 [64, 512, 576], P(('groups', 'dp')), parts along dimension 0, may hold values from -6 to 6
- lengths: int32 [64], P(('groups', 'dp')), parts along dimension 0, may hold values from 64 to 512, as said below
- w_gate: bfloat16 [7168, 8192], P(None, ('dp', 'tensor')), may hold values from -0.0625 to 0.0625
- w_up: bfloat16 [7168, 8192], P(None, ('dp', 'tensor')), may hold values from -0.0625 to 0.0625
- w_down: bfloat16 [8192, 7168], P(('dp', 'tensor')), may hold values from -0.125 to 0.125
Outputs:
- moe_out: bfloat16 [512, 7168], P(('groups', 'dp', 'tensor')), parts along dimension 0
- context: bfloat16 [64, 128, 512], P(('groups', 'dp'), 'tensor'), parts along dimension 0
The draws below stay inside these ranges and needn't reach their ends.
There are 2 independent parts, one for each index of `groups`. The reference program is written for one: setup_inputs(seed, part) draws one part's arguments, and reference() takes and returns one part's arrays. A program takes and returns all parts, laid end to end along the dimension named above; an argument that names none is the same for every part. Nothing has to cross between parts.
Inputs may be any that keep to these rules, and one draw needn't show every extreme that they name: `expert_ids`: each row names 2 different experts; at most 16 rows of one device name the same expert, and some device's rows reach that. `cap_limit`: copies beyond it, in row order within one device's rows, are dropped. `lengths`: positions 0 to length - 1 of a request are in use.
All inputs are finite; a program needn't handle non-finite values.
Results may differ from the reference program's by a relative error of at most 0.0057.
Values may be sent and summed in bfloat16 or wider, within the bound.
A program may use at most 128 MiB of HBM per device.

```python
import math
import jax
import jax.numpy as jnp
import numpy as np
from jax import lax

D = 7168
HEADS = 128
LATENT = 512
ROPE = 64
FFE = 2048
SPAN = 4
TOPK = 2
CTX = 512
ROWS_DEV = 16
ROWS = 256
REQUESTS = 32
EXPERTS = 4
CAP = 16


def shared_cache(key):
    return jax.random.truncated_normal(key, -6.0, 6.0, (REQUESTS, CTX, LATENT + ROPE), jnp.float32)


def draw_latent_cache(key, part):
    base_draw = shared_cache(key)
    return base_draw.astype(jnp.bfloat16)


def draw_queries(key, part):
    key = jax.random.fold_in(key, 23)
    fresh_draw = jax.random.truncated_normal(key, -6.0, 6.0, (REQUESTS, HEADS, LATENT + ROPE), jnp.float32)
    return fresh_draw.astype(jnp.bfloat16)


def draw_lengths(key, part):
    key = jax.random.fold_in(key, 5)
    drawn_values = jax.random.randint(key, (REQUESTS,), CTX // 8, CTX + 1, dtype=jnp.int32)
    return drawn_values.at[0].set(CTX)


def draw_cap_limit(key, part):
    key = jax.random.fold_in(key, 7)
    drawn_values = jax.random.randint(key, (EXPERTS,), (CAP + 1) // 2, CAP + 1, dtype=jnp.int32)
    return drawn_values.at[0].set(CAP)


def block_levels(rng, shape, split, smallest, top_value):
    level, own = 1.0, jax.random.fold_in(rng, 6)
    for axis_at, blocks in split:
        steps = jnp.exp(jax.random.uniform(jax.random.fold_in(own, axis_at), (blocks,), jnp.float32, smallest / len(split), top_value / len(split)))
        level = level * jnp.repeat(steps, shape[axis_at] // blocks).reshape([-1 if axis == axis_at else 1 for axis in range(len(shape))])
    return level


def routed_block(stream_key, own, number, rows, number_of, top, most, lean):
    sequence = jax.random.permutation(stream_key, number_of)
    crowded, usual = portions_of(number_of, rows * top, most, lean, True), portions_of(number_of, rows * top, most, lean, False)
    places = jnp.arange(number_of)

    def named(tallies, turn):
        used = int((tallies > 0).sum())
        fixed = max(1, used // 4)
        moved = fixed + (places - fixed + turn * (used - fixed)) % max(1, number_of - fixed)
        return jnp.zeros((number_of,), jnp.int32).at[sequence[jnp.where(places < fixed, places, moved)]].set(jnp.asarray(tallies, jnp.int32))

    tallies = jnp.where(number % 4 == 0, named(crowded, number // 4), named(usual, number - number // 4 - 1))
    mixed = jax.random.permutation(jax.random.fold_in(own, 3), number_of)
    donor, sink = mixed[0:number_of // 2 * 2:2], mixed[1:number_of // 2 * 2:2]
    slack = jnp.minimum(tallies[donor] - 1, most - tallies[sink]) // 2
    slack = jnp.where((donor == sequence[0]) | (sink == sequence[0]) | (tallies[sink] == 0), 0, jnp.maximum(slack, 0))
    moved = jax.random.randint(jax.random.fold_in(own, 4), (number_of // 2,), 0, 1 << 20) % (slack + 1)
    tallies = tallies.at[donor].add(-moved).at[sink].add(moved)
    members = jnp.searchsorted(jnp.cumsum(tallies), jnp.arange(rows * top), side="right").astype(jnp.int32)
    grid = members.reshape(top, rows).T
    grid = grid[jax.random.permutation(jax.random.fold_in(own, 1), rows)]
    turn = jax.random.randint(jax.random.fold_in(own, 2), (rows, 1), 0, top)
    return jnp.take_along_axis(grid, (jnp.arange(top)[None, :] + turn) % top, axis=1)


def portions_of(count, total, limit, lean, full):
    portions = [(1 << 20) // math.isqrt(grade ** lean) + 1 for grade in range(1, count + 1)]
    largest = limit if full else min(limit, max(-(-total // count), total * portions[0] // sum(portions)))
    least = 1 if total - largest >= count - 1 else 0
    counts, surplus = [largest] + [least] * (count - 1), total - largest - least * (count - 1)
    while surplus > 0:
        candidates = [i for i in range(1, count) if counts[i] < largest] or [i for i in range(1, count) if counts[i] < limit]
        mass, left = sum([portions[i] for i in candidates]), surplus
        for i in candidates:
            extra = min(limit - counts[i], max(1, left * portions[i] // mass), surplus)
            counts[i] = counts[i] + extra
            surplus = surplus - extra
    return np.array(counts)


def noise(own_key, shape, spread, bound, split=(), kind=jnp.bfloat16):
    gain = block_levels(own_key, shape, split, -0.22, 0.18) if split else 1.0
    entries = jax.random.normal(own_key, shape, jnp.float32) * spread * gain
    return jnp.minimum(jnp.maximum(entries, -bound), bound).astype(kind)


def setup_inputs(seed: int = 0, part: int = 0) -> dict:
    splits = jax.random.split(jax.random.key(seed), 11)
    own_keys = jax.random.split(jax.random.fold_in(splits[10], part), 11)
    token_rows = noise(own_keys[0], (ROWS, D), 1.0, 6.0, ((0, 16),))
    expert_ids_keys = jax.random.split(jax.random.fold_in(own_keys[1], 1), ROWS // ROWS_DEV)
    expert_ids_turns = jax.random.permutation(jax.random.fold_in(own_keys[1], 3), ROWS // ROWS_DEV)
    expert_ids = jax.vmap(lambda own, number: routed_block(jax.random.fold_in(own_keys[1], 2), own, number, ROWS_DEV, EXPERTS, TOPK, CAP, 2))(expert_ids_keys, expert_ids_turns).reshape((ROWS, TOPK))
    gate_weights = jnp.clip(jnp.exp(math.log(1.0) - 1.609438 * jax.random.uniform(own_keys[2], (ROWS, TOPK), jnp.float32) ** block_levels(own_keys[2], (ROWS, TOPK), ((0, 16),), -0.2, 0.2)), 0.2, 1.0)
    cap_limit = draw_cap_limit(jax.random.fold_in(jax.random.fold_in(splits[10], part), 71), part)
    queries = draw_queries(jax.random.fold_in(jax.random.fold_in(splits[10], part), 71), part)
    latent_cache = draw_latent_cache(jax.random.fold_in(jax.random.fold_in(splits[10], part), 71), part)
    lengths = draw_lengths(jax.random.fold_in(jax.random.fold_in(splits[10], part), 71), part)
    w_gate = noise(splits[7], (D, EXPERTS * FFE), D ** -0.5, 0.0625, ((1, 16),))
    w_up = noise(splits[8], (D, EXPERTS * FFE), D ** -0.5, 0.0625, ((1, 16),))
    w_down = noise(splits[9], (EXPERTS * FFE, D), FFE ** -0.5, 0.125, ((0, 16),))
    return {"token_rows": token_rows, "expert_ids": expert_ids, "gate_weights": gate_weights, "cap_limit": cap_limit, "queries": queries, "latent_cache": latent_cache, "lengths": lengths, "w_gate": w_gate, "w_up": w_up, "w_down": w_down}


score_scale = 0.07216878364870323


def route_slots(expert_ids, cap_limit):
    blocks = expert_ids.reshape(-1, ROWS_DEV * TOPK)
    onehot = (blocks[:, :, None] == jnp.arange(EXPERTS, dtype=jnp.int32)[None, None, :]).astype(jnp.int32)
    before = jnp.cumsum(onehot, axis=1) - onehot
    slot_rank = jnp.sum(before * onehot, axis=2).reshape(-1, TOPK).astype(jnp.int32)
    kept_copy = slot_rank < cap_limit[expert_ids]
    return slot_rank, kept_copy


def expert_out(operands):
    inputs, gate_cols, up_cols, down_rows = operands
    gate_part = jnp.dot(inputs, gate_cols, preferred_element_type=jnp.float32)
    up_part = jnp.dot(inputs, up_cols, preferred_element_type=jnp.float32)
    activated = (jax.nn.silu(gate_part) * up_part).astype(jnp.bfloat16)
    pieces = jnp.einsum("mjf,jfd->mjd", activated.reshape(-1, SPAN, FFE // SPAN).astype(jnp.float32),
                        down_rows.reshape(SPAN, FFE // SPAN, D).astype(jnp.float32))
    rounded = lax.optimization_barrier(pieces.astype(jnp.bfloat16))
    return jnp.sum(rounded.astype(jnp.float32), axis=1)


def attend(operands):
    query_rows, key_rows, length = operands
    scores = jnp.dot(query_rows, key_rows.T, preferred_element_type=jnp.float32) * score_scale
    in_use = jnp.arange(CTX, dtype=jnp.int32)[None, :] < length
    masked = jnp.where(in_use, scores, -1e30)
    highest = jnp.max(masked, axis=1, keepdims=True)
    weights = jnp.where(in_use, jnp.exp(masked - highest), 0.0)
    denominator = jnp.sum(weights, axis=1, keepdims=True)
    mixed_sum = jnp.dot(weights.astype(jnp.bfloat16), key_rows[:, :LATENT], preferred_element_type=jnp.float32)
    return (mixed_sum / denominator).astype(jnp.bfloat16)


def reference(token_rows, expert_ids, gate_weights, cap_limit, queries, latent_cache, lengths, w_gate, w_up, w_down):
    slot_rank, kept_copy = route_slots(expert_ids, cap_limit)
    sources = ROWS // ROWS_DEV
    source = (jnp.arange(ROWS, dtype=jnp.int32) // ROWS_DEV)[:, None]
    slot_index = jnp.where(kept_copy, source * CAP + slot_rank, sources * CAP).astype(jnp.int32)
    buffer = jnp.zeros((EXPERTS, sources * CAP, D), jnp.bfloat16)
    buffer = buffer.at[expert_ids, slot_index].set(jnp.broadcast_to(token_rows[:, None, :], (ROWS, TOPK, D)), mode="drop")
    gate_cols = w_gate.reshape(D, EXPERTS, FFE).transpose(1, 0, 2)
    up_cols = w_up.reshape(D, EXPERTS, FFE).transpose(1, 0, 2)
    down_rows = w_down.reshape(EXPERTS, FFE, D)
    outputs = lax.map(expert_out, (buffer, gate_cols, up_cols, down_rows))
    picked = outputs[expert_ids, jnp.minimum(slot_index, sources * CAP - 1)]
    factor = jnp.where(kept_copy, gate_weights, 0.0)
    moe_out = jnp.sum(factor[:, :, None] * picked, axis=1).astype(jnp.bfloat16)
    context = lax.map(attend, (queries, latent_cache, lengths))
    return (moe_out, context)
```

```python
import functools
import jax
import jax.numpy as jnp
from jax import lax
from jax.experimental import pallas as pl
from jax.experimental.pallas import tpu as pltpu
from jax.sharding import PartitionSpec as P

LATENT = 512
SPAN = 4
LANES = 128
GATHER_PARTS = 3
RETURN_PARTS = 7


score_scale = 0.07216878364870323


def expert_mlp(flat_rows, gate_cols, up_cols, down_rows):
    gate_part = jnp.dot(flat_rows, gate_cols, preferred_element_type=jnp.float32)
    up_part = jnp.dot(flat_rows, up_cols, preferred_element_type=jnp.float32)
    activated = (jax.nn.silu(gate_part) * up_part).astype(jnp.bfloat16)
    return jnp.dot(activated, down_rows, preferred_element_type=jnp.float32)


def local(
    token_rows,
    expert_ids,
    gate_weights,
    cap_limit,
    queries,
    latent_cache,
    lengths,
    w_gate,
    w_up,
    w_down,
):
    dp_count = lax.axis_size("dp")
    row_count, width = token_rows.shape
    top_count = expert_ids.shape[1]
    experts = cap_limit.shape[0]
    capacity = min(row_count, 2 * row_count * top_count * SPAN // dp_count)
    flat_ids = expert_ids.reshape(-1)
    onehot = (flat_ids[:, None] == jnp.arange(experts, dtype=jnp.int32)[None, :]).astype(jnp.int32)
    before = jnp.cumsum(onehot, axis=0) - onehot
    slot_rank = jnp.sum(before * onehot, axis=1)
    limit_copy = jnp.sum(onehot * cap_limit[None, :], axis=1)
    kept_copy = slot_rank < limit_copy
    owner_expert = jnp.arange(dp_count, dtype=jnp.int32) // SPAN
    slot_ids = jnp.arange(capacity, dtype=jnp.int32)
    pick_table = (
        (owner_expert[:, None, None] == flat_ids[None, None, :])
        & (slot_ids[None, :, None] == slot_rank[None, None, :])
        & kept_copy[None, None, :]
    )
    pick_table = pick_table.reshape(dp_count * capacity, row_count, top_count)
    send_table = jnp.any(pick_table, axis=2).astype(jnp.bfloat16)
    outgoing = jnp.dot(send_table, token_rows, preferred_element_type=jnp.float32).astype(
        jnp.bfloat16
    )
    outgoing = outgoing.reshape(dp_count, capacity, width)
    received = lax.all_to_all(outgoing, "dp", split_axis=0, concat_axis=0, tiled=True)
    shard_rows = lax.all_gather(received, "tensor", axis=0, tiled=True)
    flat_rows = shard_rows.reshape(-1, width)
    partial_terms = expert_mlp(flat_rows, w_gate, w_up, w_down).reshape(
        shard_rows.shape[0], capacity, width
    )
    owner_sum = lax.psum_scatter(partial_terms, "tensor", scatter_dimension=0, tiled=True).astype(
        jnp.bfloat16
    )
    returned = lax.all_to_all(owner_sum, "dp", split_axis=0, concat_axis=0, tiled=True).reshape(
        dp_count * capacity, width
    )
    combined = jnp.zeros((row_count, width), jnp.float32)
    for which in range(top_count):
        table = pick_table[:, :, which].T.astype(jnp.bfloat16)
        summed = jnp.dot(table, returned, preferred_element_type=jnp.float32)
        combined = combined + gate_weights[:, which : which + 1] * summed
    moe_out = combined.astype(jnp.bfloat16)
    scores = (
        jnp.einsum("rhc,rpc->rhp", queries, latent_cache, preferred_element_type=jnp.float32)
        * score_scale
    )
    positions = jnp.arange(latent_cache.shape[1], dtype=jnp.int32)
    in_use = (positions[None, :] < lengths[:, None])[:, None, :]
    masked = jnp.where(in_use, scores, -1e30)
    highest = jnp.max(masked, axis=2, keepdims=True)
    weights = jnp.where(in_use, jnp.exp(masked - highest), 0.0)
    denominator = jnp.sum(weights, axis=2, keepdims=True)
    mixed_sum = jnp.einsum(
        "rhp,rpc->rhc",
        weights.astype(jnp.bfloat16),
        latent_cache[:, :, :LATENT],
        preferred_element_type=jnp.float32,
    )
    context = (mixed_sum / denominator).astype(jnp.bfloat16)
    return (moe_out, context)


def fused_kernel(
    planes,
    gather_parts,
    return_parts,
    cap_ref,
    lengths_ref,
    rows_ref,
    ids_ref,
    gates_ref,
    queries_hbm,
    cache_hbm,
    gate_hbm,
    up_hbm,
    down_hbm,
    moe_ref,
    context_ref,
    rows_all,
    gate_w,
    up_w,
    down_w,
    queries,
    cache,
    gate_acc,
    up_acc,
    partial,
    from_core,
    from_y,
    plane_sum,
    from_below,
    from_above,
    final,
    load_sem,
    attn_sem,
    in_sem,
    up_sem,
    dn_sem,
    y_sem,
    core_sem,
    rcore_sem,
    ry_sem,
    rup_sem,
    rdn_sem,
):
    last = planes - 1
    place = lax.axis_index("dp")
    z, y, core = place // 4, (place // 2) % 2, place % 2
    dev = lambda zz, yy, cc: {"dp": zz * 4 + yy * 2 + cc}
    slot = lambda zz, yy, cc: cc * (2 * planes) + yy * planes + zz
    width = rows_ref.shape[1]
    block = rows_ref.shape[0]
    slots = 4 * planes
    part = rows_all.shape[3]
    depths = [min(part, width - part * c) for c in range(gather_parts)]
    out_part = partial.shape[3]

    attn_copies = [
        pltpu.make_async_copy(queries_hbm, queries, attn_sem.at[0]),
        pltpu.make_async_copy(cache_hbm, cache, attn_sem.at[1]),
    ]
    weight_copies = []
    for c in range(gather_parts):
        span = pl.ds(c * part, depths[c])
        weight_copies.append(pltpu.make_async_copy(gate_hbm.at[span], gate_w.at[span], load_sem.at[c]))
        weight_copies.append(pltpu.make_async_copy(up_hbm.at[span], up_w.at[span], load_sem.at[gather_parts + c]))
    down_copy = pltpu.make_async_copy(down_hbm, down_w, load_sem.at[2 * gather_parts])
    for copy in attn_copies + weight_copies + [down_copy]:
        copy.start()

    barrier = pltpu.get_barrier_semaphore()
    pl.semaphore_signal(barrier, inc=1, device_id=dev(z, 1 - y, core), device_id_type=pl.DeviceIdType.MESH)
    pl.semaphore_signal(barrier, inc=1, device_id=dev(z, y, 1 - core), device_id_type=pl.DeviceIdType.MESH)

    @pl.when(z > 0)
    def _():
        pl.semaphore_signal(barrier, inc=1, device_id=dev(z - 1, y, core), device_id_type=pl.DeviceIdType.MESH)

    @pl.when(z < last)
    def _():
        pl.semaphore_signal(barrier, inc=1, device_id=dev(z + 1, y, core), device_id_type=pl.DeviceIdType.MESH)

    own = slot(z, y, core)
    for c in range(gather_parts):
        rows_all[c, own, :, : depths[c]] = rows_ref[:, c * part : c * part + depths[c]]
    experts = cap_ref.shape[0]
    expert = lax.broadcasted_iota(jnp.int32, (8, block), 0)
    first, second = expert == ids_ref[0:1, :], expert == ids_ref[1:2, :]
    named = jnp.where(first | second, 1.0, 0.0)
    earlier = jnp.where(
        lax.broadcasted_iota(jnp.int32, (block, block), 0) < lax.broadcasted_iota(jnp.int32, (block, block), 1), 1.0, 0.0
    )
    rank = jnp.dot(named.astype(jnp.bfloat16), earlier.astype(jnp.bfloat16), preferred_element_type=jnp.float32)
    limit = jnp.zeros((8, block), jnp.float32)
    for e in range(experts):
        limit = jnp.where(expert == e, cap_ref[e].astype(jnp.float32), limit)
    weight = jnp.where(first, gates_ref[0:1, :], 0.0) + jnp.where(second, gates_ref[1:2, :], 0.0)
    weight = jnp.where(rank < limit, weight, 0.0)
    spread = jnp.zeros((block, LANES), jnp.float32)
    for term in range(3):
        rounded = weight.astype(jnp.bfloat16)
        weight = weight - rounded.astype(jnp.float32)
        to_lane = (
            lax.broadcasted_iota(jnp.int32, (8, LANES), 1) == lax.broadcasted_iota(jnp.int32, (8, LANES), 0) + 8 * term
        )
        spread = spread + lax.dot_general(
            rounded,
            jnp.where(to_lane, 1.0, 0.0).astype(jnp.bfloat16),
            (((0,), (0,)), ((), ())),
            preferred_element_type=jnp.float32,
        )
    rows_all[gather_parts - 1, own, :, depths[-1] : depths[-1] + LANES] = spread.astype(jnp.bfloat16)

    edges = jnp.where(z > 0, 1, 0) + jnp.where(z < last, 1, 0)
    pl.semaphore_wait(barrier, 2 + edges)

    def gather_copy(c, where, send, target):
        return pltpu.make_async_remote_copy(
            src_ref=rows_all.at[c, where],
            dst_ref=rows_all.at[c, where],
            send_sem=send,
            recv_sem=in_sem.at[c, where],
            device_id=target,
            device_id_type=pl.DeviceIdType.MESH,
        )

    def to_up(c, zz):
        return gather_copy(c, slot(zz, y, core), up_sem.at[c, zz], dev(z + 1, y, core))

    def to_dn(c, zz):
        return gather_copy(c, slot(zz, y, core), dn_sem.at[c, zz], dev(z - 1, y, core))

    def to_y(c, zz):
        return gather_copy(c, slot(zz, y, core), y_sem.at[c, zz], dev(z, 1 - y, core))

    def to_core(c, zz, yy):
        return gather_copy(c, slot(zz, yy, core), core_sem.at[c, yy * planes + zz], dev(z, y, 1 - core))

    def arrived(c, where):
        gather_copy(c, where, y_sem.at[c, 0], dev(z, 1 - y, core)).wait_recv()

    @pl.loop(0, gather_parts)
    def _(c):
        to_y(c, z).start()

        @pl.when(z < last)
        def _():
            to_up(c, z).start()

        @pl.when(z > 0)
        def _():
            to_dn(c, z).start()

        to_core(c, z, y).start()

    for copy in attn_copies:
        copy.wait()
    for r in range(queries.shape[0]):
        scores = (
            lax.dot_general(queries[r], cache[r], (((0,), (0,)), ((), ())), preferred_element_type=jnp.float32)
            * score_scale
        )
        in_use = lax.broadcasted_iota(jnp.int32, scores.shape, 1) < lengths_ref[r]
        masked = jnp.where(in_use, scores, -1e30)
        highest = jnp.max(masked, axis=1, keepdims=True)
        weights = jnp.where(in_use, jnp.exp(masked - highest), 0.0)
        denominator = jnp.sum(weights, axis=1, keepdims=True)
        mixed = lax.dot_general(
            weights.astype(jnp.bfloat16),
            cache[r, :LATENT, :],
            (((1,), (1,)), ((), ())),
            preferred_element_type=jnp.float32,
        )
        context_ref[r] = (mixed / denominator).astype(context_ref.dtype)

    def pass_y(c, zz):
        arrived(c, slot(zz, 1 - y, core))
        to_core(c, zz, 1 - y).start()

    def pass_y_at(c, d):
        if d == 0:
            pass_y(c, z)
            return

        @pl.when(z >= d)
        def _():
            pass_y(c, z - d)

        @pl.when(z + d <= last)
        def _():
            pass_y(c, z + d)

    for d in range(1, planes):

        @pl.loop(0, gather_parts)
        def _(c, d=d):
            @pl.when(z >= d)
            def _():
                arrived(c, slot(z - d, y, core))

                @pl.when(z < last)
                def _():
                    to_up(c, z - d).start()

                to_y(c, z - d).start()
                to_core(c, z - d, y).start()

            @pl.when(z + d <= last)
            def _():
                arrived(c, slot(z + d, y, core))

                @pl.when(z > 0)
                def _():
                    to_dn(c, z + d).start()

                to_y(c, z + d).start()
                to_core(c, z + d, y).start()

            pass_y_at(c, d - 1)

    for c in range(gather_parts):
        pass_y_at(c, last)
        for yy in range(2):
            for zz in range(planes):
                arrived(c, slot(zz, yy, 1 - core))
        weight_copies[2 * c].wait()
        weight_copies[2 * c + 1].wait()
        span = pl.ds(c * part, depths[c])
        rows = rows_all[c, :, :, : depths[c]].reshape(slots * block, depths[c])
        gate_part = jnp.dot(rows, gate_w[span], preferred_element_type=jnp.float32)
        up_part = jnp.dot(rows, up_w[span], preferred_element_type=jnp.float32)
        if c > 0:
            gate_part, up_part = gate_part + gate_acc[...], up_part + up_acc[...]
        if c < gather_parts - 1:
            gate_acc[...] = gate_part
            up_acc[...] = up_part
    activated = ((gate_part / (1.0 + jnp.exp(-gate_part))) * up_part).astype(jnp.bfloat16)
    terms = rows_all[gather_parts - 1, :, :, depths[-1] : depths[-1] + LANES].reshape(slots * block, LANES)
    lane = lax.broadcasted_iota(jnp.int32, (slots * block, LANES), 1)
    factor = jnp.sum(
        jnp.where((lane == z) | (lane == z + 8) | (lane == z + 16), terms.astype(jnp.float32), 0.0), axis=1, keepdims=True
    )
    down_copy.wait()

    half = 2 * planes

    def core_copy(c):
        return pltpu.make_async_remote_copy(
            src_ref=partial.at[c, pl.ds((1 - core) * half, half)],
            dst_ref=from_core.at[c],
            send_sem=rcore_sem.at[0, c],
            recv_sem=rcore_sem.at[1, c],
            device_id=dev(z, y, 1 - core),
            device_id_type=pl.DeviceIdType.MESH,
        )

    def y_copy(c):
        return pltpu.make_async_remote_copy(
            src_ref=from_core.at[c, pl.ds((1 - y) * planes, planes)],
            dst_ref=from_y.at[c],
            send_sem=ry_sem.at[0, c],
            recv_sem=ry_sem.at[1, c],
            device_id=dev(z, 1 - y, core),
            device_id_type=pl.DeviceIdType.MESH,
        )

    def z_copy(src, dst, sem, c, k, target):
        return pltpu.make_async_remote_copy(
            src_ref=src.at[c, k],
            dst_ref=dst.at[c, k],
            send_sem=sem.at[0, c, k],
            recv_sem=sem.at[1, c, k],
            device_id=target,
            device_id_type=pl.DeviceIdType.MESH,
        )

    def up_copy(c, k, src):
        return z_copy(src, from_below, rup_sem, c, k, dev(z + 1, y, core))

    def dn_copy(c, k, src):
        return z_copy(src, from_above, rdn_sem, c, k, dev(z - 1, y, core))

    f32 = lambda value: value.astype(jnp.float32)

    def join_core(c):
        core_copy(c).wait_recv()
        far = pl.ds((1 - y) * planes, planes)
        mine = partial[c, pl.ds(core * half + (1 - y) * planes, planes)]
        from_core[c, far] = (f32(mine) + f32(from_core[c, far])).astype(jnp.bfloat16)
        y_copy(c).start()

    for c in range(return_parts):
        result = jnp.dot(
            activated, down_w[:, c * out_part : (c + 1) * out_part], preferred_element_type=jnp.float32
        )
        partial[c] = (result * factor).astype(jnp.bfloat16).reshape(slots, block, out_part)
        core_copy(c).start()
        if c > 0:
            join_core(c - 1)
    join_core(return_parts - 1)

    def hop(c, k, held, sem, copy):
        z_copy(plane_sum, held, sem, c, k, dev(z, 1 - y, core)).wait_recv()
        held[c, k] = (f32(held[c, k]) + f32(plane_sum[c, k])).astype(jnp.bfloat16)
        copy(c, k, held).start()

    @pl.loop(0, return_parts + last)
    def _(t):
        c_up = t - z

        @pl.when((z > 0) & (c_up >= 0) & (c_up < return_parts))
        def _():
            for k in range(last, 0, -1):

                @pl.when(z < k)
                def _():
                    hop(c_up, k, from_below, rup_sem, up_copy)

        c_dn = t - (last - z)

        @pl.when((z < last) & (c_dn >= 0) & (c_dn < return_parts))
        def _():
            for k in range(last):

                @pl.when(z > k)
                def _():
                    hop(c_dn, k, from_above, rdn_sem, dn_copy)

        @pl.when(t < return_parts)
        def _():
            y_copy(t).wait_recv()
            near = pl.ds(y * planes, planes)
            mine = partial[t, pl.ds(core * half + y * planes, planes)]
            plane_sum[t] = (f32(mine) + f32(from_core[t, near]) + f32(from_y[t])).astype(jnp.bfloat16)

            @pl.when(z == 0)
            def _():
                for k in range(last, 0, -1):
                    up_copy(t, k, plane_sum).start()

            @pl.when(z == last)
            def _():
                for k in range(last):
                    dn_copy(t, k, plane_sum).start()

    for c in range(return_parts):
        final[...] = f32(plane_sum[c, z])

        @pl.when(z > 0)
        def _():
            up_copy(c, z, plane_sum).wait_recv()
            final[...] += f32(from_below[c, z])

        @pl.when(z < last)
        def _():
            dn_copy(c, z, plane_sum).wait_recv()
            final[...] += f32(from_above[c, z])

        moe_ref[:, c * out_part : (c + 1) * out_part] = final[...].astype(moe_ref.dtype)

    @pl.loop(0, gather_parts)
    def _(c):
        for zz in range(planes):
            to_y(c, zz).wait_send()
            to_core(c, zz, 0).wait_send()
            to_core(c, zz, 1).wait_send()

            @pl.when((z >= zz) & (z < last))
            def _():
                to_up(c, zz).wait_send()

            @pl.when((z <= zz) & (z > 0))
            def _():
                to_dn(c, zz).wait_send()

    @pl.loop(0, return_parts)
    def _(c):
        core_copy(c).wait_send()
        y_copy(c).wait_send()
        for k in range(planes):

            @pl.when(z < k)
            def _():
                up_copy(c, k, plane_sum).wait_send()

            @pl.when(z > k)
            def _():
                dn_copy(c, k, plane_sum).wait_send()


def local_fused(
    token_rows,
    expert_ids,
    gate_weights,
    cap_limit,
    queries,
    latent_cache,
    lengths,
    w_gate,
    w_up,
    w_down,
):
    dp_count = lax.axis_size("dp")
    planes = dp_count // SPAN
    row_count, width = token_rows.shape
    hidden = w_gate.shape[1]
    requests, heads = queries.shape[:2]
    total = row_count * dp_count
    gather_parts, return_parts = GATHER_PARTS, RETURN_PARTS
    part = -(-(width + LANES) // (gather_parts * LANES)) * LANES
    out_part = width // return_parts
    bf16, f32 = jnp.bfloat16, jnp.float32
    any_space = pl.BlockSpec(memory_space=pl.ANY)
    vmem = pl.BlockSpec(memory_space=pltpu.VMEM)
    smem = pl.BlockSpec(memory_space=pltpu.SMEM)
    dma = pltpu.SemaphoreType.DMA
    queries_t = jnp.swapaxes(queries, 1, 2)
    cache_t = jnp.swapaxes(latent_cache, 1, 2)
    back = lambda count: pltpu.VMEM((return_parts, count, row_count, out_part), bf16)
    return pl.pallas_call(
        functools.partial(fused_kernel, planes, gather_parts, return_parts),
        out_shape=(
            jax.ShapeDtypeStruct((row_count, width), bf16),
            jax.ShapeDtypeStruct((requests, heads, LATENT), bf16),
        ),
        in_specs=[smem, smem, vmem, vmem, vmem] + [any_space] * 5,
        out_specs=(vmem, vmem),
        scratch_shapes=[
            pltpu.VMEM((gather_parts, dp_count, row_count, part), bf16),
            pltpu.VMEM(w_gate.shape, bf16),
            pltpu.VMEM(w_up.shape, bf16),
            pltpu.VMEM(w_down.shape, bf16),
            pltpu.VMEM(queries_t.shape, bf16),
            pltpu.VMEM(cache_t.shape, bf16),
            pltpu.VMEM((total, hidden), f32),
            pltpu.VMEM((total, hidden), f32),
            back(dp_count),
            back(2 * planes),
            back(planes),
            back(planes),
            back(planes),
            back(planes),
            pltpu.VMEM((row_count, out_part), f32),
            dma((2 * gather_parts + 1,)),
            dma((2,)),
            dma((gather_parts, dp_count)),
            dma((gather_parts, planes)),
            dma((gather_parts, planes)),
            dma((gather_parts, planes)),
            dma((gather_parts, 2 * planes)),
            dma((2, return_parts)),
            dma((2, return_parts)),
            dma((2, return_parts, planes)),
            dma((2, return_parts, planes)),
        ],
        compiler_params=pltpu.CompilerParams(
            collective_id=0, has_side_effects=True, vmem_limit_bytes=58 * 1024 * 1024
        ),
        cost_estimate=pl.CostEstimate(
            flops=6 * total * width * hidden, bytes_accessed=6 * width * hidden, transcendentals=total * hidden
        ),
    )(cap_limit, lengths, token_rows, expert_ids.T, gate_weights.T, queries_t, cache_t, w_gate, w_up, w_down)


def solution(mesh):
    in_specs = (
        P(("groups", "dp", "tensor"), None),
        P(("groups", "dp", "tensor"), None),
        P(("groups", "dp", "tensor"), None),
        P("groups"),
        P(("groups", "dp"), "tensor", None),
        P(("groups", "dp"), None, None),
        P(("groups", "dp")),
        P(None, ("dp", "tensor")),
        P(None, ("dp", "tensor")),
        P(("dp", "tensor"), None),
    )
    out_specs = (P(("groups", "dp", "tensor"), None), P(("groups", "dp"), "tensor", None))
    planes = mesh.shape["dp"] // SPAN
    fits = mesh.shape["tensor"] == 1 and mesh.shape["dp"] % SPAN == 0 and 2 <= planes <= 4
    body = local_fused if fits else local
    return jax.shard_map(body, mesh=mesh, in_specs=in_specs, out_specs=out_specs, check_vma=False)
```

```python
import functools
import jax
import jax.numpy as jnp
from jax import lax
from jax.experimental import pallas as pl
from jax.experimental.pallas import tpu as pltpu
from jax.sharding import PartitionSpec as P

LATENT = 512
SPAN = 4
LANES = 128
GATHER_PARTS = 3
RETURN_PARTS = 7


score_scale = 0.07216878364870323


def expert_mlp(flat_rows, gate_cols, up_cols, down_rows):
    gate_part = jnp.dot(flat_rows, gate_cols, preferred_element_type=jnp.float32)
    up_part = jnp.dot(flat_rows, up_cols, preferred_element_type=jnp.float32)
    activated = (jax.nn.silu(gate_part) * up_part).astype(jnp.bfloat16)
    return jnp.dot(activated, down_rows, preferred_element_type=jnp.float32)


def local(
    token_rows,
    expert_ids,
    gate_weights,
    cap_limit,
    queries,
    latent_cache,
    lengths,
    w_gate,
    w_up,
    w_down,
):
    dp_count = lax.axis_size("dp")
    row_count, width = token_rows.shape
    top_count = expert_ids.shape[1]
    experts = cap_limit.shape[0]
    capacity = min(row_count, 2 * row_count * top_count * SPAN // dp_count)
    flat_ids = expert_ids.reshape(-1)
    onehot = (flat_ids[:, None] == jnp.arange(experts, dtype=jnp.int32)[None, :]).astype(jnp.int32)
    before = jnp.cumsum(onehot, axis=0) - onehot
    slot_rank = jnp.sum(before * onehot, axis=1)
    limit_copy = jnp.sum(onehot * cap_limit[None, :], axis=1)
    kept_copy = slot_rank < limit_copy
    owner_expert = jnp.arange(dp_count, dtype=jnp.int32) // SPAN
    slot_ids = jnp.arange(capacity, dtype=jnp.int32)
    pick_table = (
        (owner_expert[:, None, None] == flat_ids[None, None, :])
        & (slot_ids[None, :, None] == slot_rank[None, None, :])
        & kept_copy[None, None, :]
    )
    pick_table = pick_table.reshape(dp_count * capacity, row_count, top_count)
    send_table = jnp.any(pick_table, axis=2).astype(jnp.bfloat16)
    outgoing = jnp.dot(send_table, token_rows, preferred_element_type=jnp.float32).astype(
        jnp.bfloat16
    )
    outgoing = outgoing.reshape(dp_count, capacity, width)
    received = lax.all_to_all(outgoing, "dp", split_axis=0, concat_axis=0, tiled=True)
    shard_rows = lax.all_gather(received, "tensor", axis=0, tiled=True)
    flat_rows = shard_rows.reshape(-1, width)
    partial_terms = expert_mlp(flat_rows, w_gate, w_up, w_down).reshape(
        shard_rows.shape[0], capacity, width
    )
    owner_sum = lax.psum_scatter(partial_terms, "tensor", scatter_dimension=0, tiled=True).astype(
        jnp.bfloat16
    )
    returned = lax.all_to_all(owner_sum, "dp", split_axis=0, concat_axis=0, tiled=True).reshape(
        dp_count * capacity, width
    )
    combined = jnp.zeros((row_count, width), jnp.float32)
    for which in range(top_count):
        table = pick_table[:, :, which].T.astype(jnp.bfloat16)
        summed = jnp.dot(table, returned, preferred_element_type=jnp.float32)
        combined = combined + gate_weights[:, which : which + 1] * summed
    moe_out = combined.astype(jnp.bfloat16)
    scores = (
        jnp.einsum("rhc,rpc->rhp", queries, latent_cache, preferred_element_type=jnp.float32)
        * score_scale
    )
    positions = jnp.arange(latent_cache.shape[1], dtype=jnp.int32)
    in_use = (positions[None, :] < lengths[:, None])[:, None, :]
    masked = jnp.where(in_use, scores, -1e30)
    highest = jnp.max(masked, axis=2, keepdims=True)
    weights = jnp.where(in_use, jnp.exp(masked - highest), 0.0)
    denominator = jnp.sum(weights, axis=2, keepdims=True)
    mixed_sum = jnp.einsum(
        "rhp,rpc->rhc",
        weights.astype(jnp.bfloat16),
        latent_cache[:, :, :LATENT],
        preferred_element_type=jnp.float32,
    )
    context = (mixed_sum / denominator).astype(jnp.bfloat16)
    return (moe_out, context)


def fused_kernel(
    planes,
    gather_parts,
    return_parts,
    cap_ref,
    lengths_ref,
    rows_ref,
    ids_ref,
    gates_ref,
    queries_hbm,
    cache_hbm,
    gate_hbm,
    up_hbm,
    down_hbm,
    moe_ref,
    context_ref,
    rows_all,
    gate_w,
    up_w,
    down_w,
    queries,
    cache,
    gate_acc,
    up_acc,
    partial,
    from_core,
    from_y,
    plane_sum,
    from_planes,
    load_sem,
    attn_sem,
    in_sem,
    up_sem,
    dn_sem,
    y_sem,
    core_sem,
    rcore_sem,
    ry_sem,
    rz_sem,
):
    last = planes - 1
    place = lax.axis_index("dp")
    z, y, core = place // 4, (place // 2) % 2, place % 2
    dev = lambda zz, yy, cc: {"dp": zz * 4 + yy * 2 + cc}
    slot = lambda zz, yy, cc: cc * (2 * planes) + yy * planes + zz
    width = rows_ref.shape[1]
    block = rows_ref.shape[0]
    slots = 4 * planes
    part = rows_all.shape[3]
    depths = [min(part, width - part * c) for c in range(gather_parts)]
    out_part = partial.shape[3]

    attn_copies = [
        pltpu.make_async_copy(queries_hbm, queries, attn_sem.at[0]),
        pltpu.make_async_copy(cache_hbm, cache, attn_sem.at[1]),
    ]
    weight_copies = []
    for c in range(gather_parts):
        span = pl.ds(c * part, depths[c])
        weight_copies.append(pltpu.make_async_copy(gate_hbm.at[span], gate_w.at[span], load_sem.at[c]))
        weight_copies.append(pltpu.make_async_copy(up_hbm.at[span], up_w.at[span], load_sem.at[gather_parts + c]))
    down_copy = pltpu.make_async_copy(down_hbm, down_w, load_sem.at[2 * gather_parts])
    for copy in attn_copies + weight_copies + [down_copy]:
        copy.start()

    barrier = pltpu.get_barrier_semaphore()
    pl.semaphore_signal(barrier, inc=1, device_id=dev(z, 1 - y, core), device_id_type=pl.DeviceIdType.MESH)
    pl.semaphore_signal(barrier, inc=1, device_id=dev(z, y, 1 - core), device_id_type=pl.DeviceIdType.MESH)

    for d in range(1, planes):
        pl.semaphore_signal(
            barrier, inc=1, device_id=dev((z + d) % planes, y, core), device_id_type=pl.DeviceIdType.MESH
        )

    own = slot(z, y, core)
    for c in range(gather_parts):
        rows_all[c, own, :, : depths[c]] = rows_ref[:, c * part : c * part + depths[c]]
    experts = cap_ref.shape[0]
    expert = lax.broadcasted_iota(jnp.int32, (8, block), 0)
    first, second = expert == ids_ref[0:1, :], expert == ids_ref[1:2, :]
    named = jnp.where(first | second, 1.0, 0.0)
    earlier = jnp.where(
        lax.broadcasted_iota(jnp.int32, (block, block), 0) < lax.broadcasted_iota(jnp.int32, (block, block), 1), 1.0, 0.0
    )
    rank = jnp.dot(named.astype(jnp.bfloat16), earlier.astype(jnp.bfloat16), preferred_element_type=jnp.float32)
    limit = jnp.zeros((8, block), jnp.float32)
    for e in range(experts):
        limit = jnp.where(expert == e, cap_ref[e].astype(jnp.float32), limit)
    weight = jnp.where(first, gates_ref[0:1, :], 0.0) + jnp.where(second, gates_ref[1:2, :], 0.0)
    weight = jnp.where(rank < limit, weight, 0.0)
    spread = jnp.zeros((block, LANES), jnp.float32)
    for term in range(3):
        rounded = weight.astype(jnp.bfloat16)
        weight = weight - rounded.astype(jnp.float32)
        to_lane = (
            lax.broadcasted_iota(jnp.int32, (8, LANES), 1) == lax.broadcasted_iota(jnp.int32, (8, LANES), 0) + 8 * term
        )
        spread = spread + lax.dot_general(
            rounded,
            jnp.where(to_lane, 1.0, 0.0).astype(jnp.bfloat16),
            (((0,), (0,)), ((), ())),
            preferred_element_type=jnp.float32,
        )
    rows_all[gather_parts - 1, own, :, depths[-1] : depths[-1] + LANES] = spread.astype(jnp.bfloat16)

    pl.semaphore_wait(barrier, 2 + last)

    def gather_copy(c, where, send, target):
        return pltpu.make_async_remote_copy(
            src_ref=rows_all.at[c, where],
            dst_ref=rows_all.at[c, where],
            send_sem=send,
            recv_sem=in_sem.at[c, where],
            device_id=target,
            device_id_type=pl.DeviceIdType.MESH,
        )

    def to_up(c, zz):
        return gather_copy(c, slot(zz, y, core), up_sem.at[c, zz], dev(z + 1, y, core))

    def to_dn(c, zz):
        return gather_copy(c, slot(zz, y, core), dn_sem.at[c, zz], dev(z - 1, y, core))

    def to_y(c, zz):
        return gather_copy(c, slot(zz, y, core), y_sem.at[c, zz], dev(z, 1 - y, core))

    def to_core(c, zz, yy):
        return gather_copy(c, slot(zz, yy, core), core_sem.at[c, yy * planes + zz], dev(z, y, 1 - core))

    def arrived(c, where):
        gather_copy(c, where, y_sem.at[c, 0], dev(z, 1 - y, core)).wait_recv()

    @pl.loop(0, gather_parts)
    def _(c):
        to_y(c, z).start()

        @pl.when(z < last)
        def _():
            to_up(c, z).start()

        @pl.when(z > 0)
        def _():
            to_dn(c, z).start()

        to_core(c, z, y).start()

    for copy in attn_copies:
        copy.wait()
    for r in range(queries.shape[0]):
        scores = (
            lax.dot_general(queries[r], cache[r], (((0,), (0,)), ((), ())), preferred_element_type=jnp.float32)
            * score_scale
        )
        in_use = lax.broadcasted_iota(jnp.int32, scores.shape, 1) < lengths_ref[r]
        masked = jnp.where(in_use, scores, -1e30)
        highest = jnp.max(masked, axis=1, keepdims=True)
        weights = jnp.where(in_use, jnp.exp(masked - highest), 0.0)
        denominator = jnp.sum(weights, axis=1, keepdims=True)
        mixed = lax.dot_general(
            weights.astype(jnp.bfloat16),
            cache[r, :LATENT, :],
            (((1,), (1,)), ((), ())),
            preferred_element_type=jnp.float32,
        )
        context_ref[r] = (mixed / denominator).astype(context_ref.dtype)

    def pass_y(c, zz):
        arrived(c, slot(zz, 1 - y, core))
        to_core(c, zz, 1 - y).start()

    def pass_y_at(c, d):
        if d == 0:
            pass_y(c, z)
            return

        @pl.when(z >= d)
        def _():
            pass_y(c, z - d)

        @pl.when(z + d <= last)
        def _():
            pass_y(c, z + d)

    for d in range(1, planes):

        @pl.loop(0, gather_parts)
        def _(c, d=d):
            @pl.when(z >= d)
            def _():
                arrived(c, slot(z - d, y, core))

                @pl.when(z < last)
                def _():
                    to_up(c, z - d).start()

                to_y(c, z - d).start()
                to_core(c, z - d, y).start()

            @pl.when(z + d <= last)
            def _():
                arrived(c, slot(z + d, y, core))

                @pl.when(z > 0)
                def _():
                    to_dn(c, z + d).start()

                to_y(c, z + d).start()
                to_core(c, z + d, y).start()

            pass_y_at(c, d - 1)

    for c in range(gather_parts):
        pass_y_at(c, last)
        for yy in range(2):
            for zz in range(planes):
                arrived(c, slot(zz, yy, 1 - core))
        weight_copies[2 * c].wait()
        weight_copies[2 * c + 1].wait()
        span = pl.ds(c * part, depths[c])
        rows = rows_all[c, :, :, : depths[c]].reshape(slots * block, depths[c])
        gate_part = jnp.dot(rows, gate_w[span], preferred_element_type=jnp.float32)
        up_part = jnp.dot(rows, up_w[span], preferred_element_type=jnp.float32)
        if c > 0:
            gate_part, up_part = gate_part + gate_acc[...], up_part + up_acc[...]
        if c < gather_parts - 1:
            gate_acc[...] = gate_part
            up_acc[...] = up_part
    activated = ((gate_part / (1.0 + jnp.exp(-gate_part))) * up_part).astype(jnp.bfloat16)
    terms = rows_all[gather_parts - 1, :, :, depths[-1] : depths[-1] + LANES].reshape(slots * block, LANES)
    lane = lax.broadcasted_iota(jnp.int32, (slots * block, LANES), 1)
    factor = jnp.sum(
        jnp.where((lane == z) | (lane == z + 8) | (lane == z + 16), terms.astype(jnp.float32), 0.0), axis=1, keepdims=True
    )
    down_copy.wait()

    half = 2 * planes

    def core_copy(c):
        return pltpu.make_async_remote_copy(
            src_ref=partial.at[c, pl.ds((1 - core) * half, half)],
            dst_ref=from_core.at[c],
            send_sem=rcore_sem.at[0, c],
            recv_sem=rcore_sem.at[1, c],
            device_id=dev(z, y, 1 - core),
            device_id_type=pl.DeviceIdType.MESH,
        )

    def y_copy(c):
        return pltpu.make_async_remote_copy(
            src_ref=from_core.at[c, pl.ds((1 - y) * planes, planes)],
            dst_ref=from_y.at[c],
            send_sem=ry_sem.at[0, c],
            recv_sem=ry_sem.at[1, c],
            device_id=dev(z, 1 - y, core),
            device_id_type=pl.DeviceIdType.MESH,
        )

    def z_copy(c, k):
        return pltpu.make_async_remote_copy(
            src_ref=plane_sum.at[c, k],
            dst_ref=from_planes.at[c, z],
            send_sem=rz_sem.at[0, c, k],
            recv_sem=rz_sem.at[1, c, z],
            device_id=dev(k, y, core),
            device_id_type=pl.DeviceIdType.MESH,
        )

    def z_arrival(c, k):
        return pltpu.make_async_remote_copy(
            src_ref=plane_sum.at[c, z],
            dst_ref=from_planes.at[c, k],
            send_sem=rz_sem.at[0, c, k],
            recv_sem=rz_sem.at[1, c, k],
            device_id=dev(k, y, core),
            device_id_type=pl.DeviceIdType.MESH,
        )

    f32 = lambda value: value.astype(jnp.float32)

    def join_core(c):
        core_copy(c).wait_recv()
        far = pl.ds((1 - y) * planes, planes)
        mine = partial[c, pl.ds(core * half + (1 - y) * planes, planes)]
        from_core[c, far] = (f32(mine) + f32(from_core[c, far])).astype(jnp.bfloat16)
        y_copy(c).start()

    for c in range(return_parts):
        result = jnp.dot(
            activated, down_w[:, c * out_part : (c + 1) * out_part], preferred_element_type=jnp.float32
        )
        partial[c] = (result * factor).astype(jnp.bfloat16).reshape(slots, block, out_part)
        core_copy(c).start()
        if c > 0:
            join_core(c - 1)
    join_core(return_parts - 1)

    others = [(z + d) % planes for d in range(1, planes)]

    @pl.loop(0, return_parts)
    def _(c):
        y_copy(c).wait_recv()
        near = pl.ds(y * planes, planes)
        mine = partial[c, pl.ds(core * half + y * planes, planes)]
        plane_sum[c] = (f32(mine) + f32(from_core[c, near]) + f32(from_y[c])).astype(jnp.bfloat16)
        for k in others:
            z_copy(c, k).start()

    for c in range(return_parts):
        final = f32(plane_sum[c, z])
        for k in others:
            z_arrival(c, k).wait_recv()
            final = final + f32(from_planes[c, k])
        moe_ref[:, c * out_part : (c + 1) * out_part] = final.astype(moe_ref.dtype)

    @pl.loop(0, gather_parts)
    def _(c):
        for zz in range(planes):
            to_y(c, zz).wait_send()
            to_core(c, zz, 0).wait_send()
            to_core(c, zz, 1).wait_send()

            @pl.when((z >= zz) & (z < last))
            def _():
                to_up(c, zz).wait_send()

            @pl.when((z <= zz) & (z > 0))
            def _():
                to_dn(c, zz).wait_send()

    @pl.loop(0, return_parts)
    def _(c):
        core_copy(c).wait_send()
        y_copy(c).wait_send()
        for k in others:
            z_copy(c, k).wait_send()


def place_kernel(moe_in, context_in, moe_out, context_out, sem):
    copies = [
        pltpu.make_async_copy(moe_in, moe_out, sem.at[0]),
        pltpu.make_async_copy(context_in, context_out, sem.at[1]),
    ]
    for copy in copies:
        copy.start()
    for copy in copies:
        copy.wait()


def local_fused(
    token_rows,
    expert_ids,
    gate_weights,
    cap_limit,
    queries,
    latent_cache,
    lengths,
    w_gate,
    w_up,
    w_down,
):
    dp_count = lax.axis_size("dp")
    planes = dp_count // SPAN
    row_count, width = token_rows.shape
    hidden = w_gate.shape[1]
    requests, heads = queries.shape[:2]
    total = row_count * dp_count
    gather_parts, return_parts = GATHER_PARTS, RETURN_PARTS
    part = -(-(width + LANES) // (gather_parts * LANES)) * LANES
    out_part = width // return_parts
    bf16, f32 = jnp.bfloat16, jnp.float32
    any_space = pl.BlockSpec(memory_space=pl.ANY)
    vmem = pl.BlockSpec(memory_space=pltpu.VMEM)
    smem = pl.BlockSpec(memory_space=pltpu.SMEM)
    dma = pltpu.SemaphoreType.DMA
    queries_t = jnp.swapaxes(queries, 1, 2)
    cache_t = jnp.swapaxes(latent_cache, 1, 2)
    back = lambda count: pltpu.VMEM((return_parts, count, row_count, out_part), bf16)
    results = pl.pallas_call(
        functools.partial(fused_kernel, planes, gather_parts, return_parts),
        out_shape=(
            jax.ShapeDtypeStruct((row_count, width), bf16),
            jax.ShapeDtypeStruct((requests, heads, LATENT), bf16),
        ),
        in_specs=[smem, smem, vmem, vmem, vmem] + [any_space] * 5,
        out_specs=(vmem, vmem),
        scratch_shapes=[
            pltpu.VMEM((gather_parts, dp_count, row_count, part), bf16),
            pltpu.VMEM(w_gate.shape, bf16),
            pltpu.VMEM(w_up.shape, bf16),
            pltpu.VMEM(w_down.shape, bf16),
            pltpu.VMEM(queries_t.shape, bf16),
            pltpu.VMEM(cache_t.shape, bf16),
            pltpu.VMEM((total, hidden), f32),
            pltpu.VMEM((total, hidden), f32),
            back(dp_count),
            back(2 * planes),
            back(planes),
            back(planes),
            back(planes),
            dma((2 * gather_parts + 1,)),
            dma((2,)),
            dma((gather_parts, dp_count)),
            dma((gather_parts, planes)),
            dma((gather_parts, planes)),
            dma((gather_parts, planes)),
            dma((gather_parts, 2 * planes)),
            dma((2, return_parts)),
            dma((2, return_parts)),
            dma((2, return_parts, planes)),
        ],
        compiler_params=pltpu.CompilerParams(
            collective_id=0, has_side_effects=True, vmem_limit_bytes=58 * 1024 * 1024
        ),
        cost_estimate=pl.CostEstimate(
            flops=6 * total * width * hidden, bytes_accessed=6 * width * hidden, transcendentals=total * hidden
        ),
    )(cap_limit, lengths, token_rows, expert_ids.T, gate_weights.T, queries_t, cache_t, w_gate, w_up, w_down)
    return pl.pallas_call(
        place_kernel,
        out_shape=tuple(jax.ShapeDtypeStruct(r.shape, r.dtype) for r in results),
        in_specs=[vmem, vmem],
        out_specs=(any_space, any_space),
        scratch_shapes=[dma((2,))],
    )(*results)


def solution(mesh):
    in_specs = (
        P(("groups", "dp", "tensor"), None),
        P(("groups", "dp", "tensor"), None),
        P(("groups", "dp", "tensor"), None),
        P("groups"),
        P(("groups", "dp"), "tensor", None),
        P(("groups", "dp"), None, None),
        P(("groups", "dp")),
        P(None, ("dp", "tensor")),
        P(None, ("dp", "tensor")),
        P(("dp", "tensor"), None),
    )
    out_specs = (P(("groups", "dp", "tensor"), None), P(("groups", "dp"), "tensor", None))
    planes = mesh.shape["dp"] // SPAN
    fits = mesh.shape["tensor"] == 1 and mesh.shape["dp"] % SPAN == 0 and 2 <= planes <= 4
    body = local_fused if fits else local
    return jax.shard_map(body, mesh=mesh, in_specs=in_specs, out_specs=out_specs, check_vma=False)
```
